128 devices in a mesh: node: 8 (over z, core), local: 16 (over x, y).
Axes of the slice: x: 4, y: 4, z: 4, core: 2. Of those that a mesh axis runs over, the one named last changes fastest.
Arguments:
- activations: bfloat16 [1024, 7168], P(('node', 'local')), may hold values from -6 to 6
- expert_ids: int32 [1024, 8], P(('node', 'local')), may hold values from 0 to 31, all different within a row; in each aligned block of 8 rows (0 to 7, 8 to 15, ...) at most 4 rows name the same one
- route_weights: bfloat16 [1024, 8], P(('node', 'local')), may hold values from 0.099609375 to 0.5
- w_gate: bfloat16 [32, 7168, 2048], P('local', None, 'node'), may hold values from -0.0625 to 0.0625
- w_up: bfloat16 [32, 7168, 2048], P('local', None, 'node'), may hold values from -0.0625 to 0.0625
- w_down: bfloat16 [32, 2048, 7168], P('local', 'node'), may hold values from -0.125 to 0.125
Outputs:
- combined: bfloat16 [1024, 7168], P(('node', 'local'))
The draws below stay inside these ranges and needn't reach their ends.
Inputs may be any that keep to these rules, and one draw needn't show every extreme that they name: `expert_ids`: each row names 8 different experts. Among the 8 rows of one device no expert is named by more than 4 rows, a bound that some block reaches.
All inputs are finite; a program needn't handle non-finite values.
Results may differ from the reference program's by a relative error of at most 0.02.
Values may be sent and summed in bfloat16 or wider, within the bound.
A program may use at most 192 MiB of HBM per device.

```python
import math
import jax
import jax.numpy as jnp
import numpy as np
from jax import lax

D = 7168
FF = 2048
TOPK = 8
TOK_DEV = 8
EXPERTS = 32
MOST = 4
TOKENS = 1024
N_NODE = 8
N_LOCAL = 16


def level_of(stream_key, extent, split, low, top_value):
    gain = 1.0
    for position, shards_of in split:
        heights = jax.random.uniform(jax.random.fold_in(jax.random.fold_in(stream_key, 6), position), (shards_of,), jnp.float32, low / len(split), top_value / len(split))
        gain = gain * jnp.repeat(jnp.exp(heights), extent[position] // shards_of).reshape((-1,) + (1,) * (len(extent) - 1 - position))
    return gain


def deal_out(rng, own, number, rows, count, top, bound, slope):
    sequence = jax.random.permutation(rng, count)
    crowded, ordinary = load_shares(count, rows * top, bound, slope, True), load_shares(count, rows * top, bound, slope, False)
    places = jnp.arange(count)

    def named(tallies, turn):
        used = int((tallies > 0).sum())
        fixed = max(1, used // 4)
        passed = fixed + (places - fixed + turn * (used - fixed)) % max(1, count - fixed)
        return jnp.zeros((count,), jnp.int32).at[sequence[jnp.where(places < fixed, places, passed)]].set(jnp.asarray(tallies, jnp.int32))

    tallies = jnp.where(number % 4 == 0, named(crowded, number // 4), named(ordinary, number - number // 4 - 1))
    mixed = jax.random.permutation(jax.random.fold_in(own, 3), count)
    donor, receiver = mixed[0:count // 2 * 2:2], mixed[1:count // 2 * 2:2]
    room = jnp.minimum(tallies[donor] - 1, bound - tallies[receiver]) // 2
    room = jnp.where((donor == sequence[0]) | (receiver == sequence[0]) | (tallies[receiver] == 0), 0, jnp.maximum(room, 0))
    passed = jax.random.randint(jax.random.fold_in(own, 4), (count // 2,), 0, 1 << 20) % (room + 1)
    tallies = tallies.at[donor].add(-passed).at[receiver].add(passed)
    members = jnp.searchsorted(jnp.cumsum(tallies), jnp.arange(rows * top), side="right").astype(jnp.int32)
    table = members.reshape(top, rows).T
    table = table[jax.random.permutation(jax.random.fold_in(own, 1), rows)]
    turn = jax.random.randint(jax.random.fold_in(own, 2), (rows, 1), 0, top)
    return jnp.take_along_axis(table, (jnp.arange(top)[None, :] + turn) % top, axis=1)


def load_shares(number_of, total, most, skew, full):
    loads = [(1 << 20) // math.isqrt(grade ** skew) + 1 for grade in range(1, number_of + 1)]
    largest = most if full else min(most, max(-(-total // number_of), total * loads[0] // sum(loads)))
    least = 1 if total - largest >= number_of - 1 else 0
    holding, spare = [largest] + [least] * (number_of - 1), total - largest - least * (number_of - 1)
    while spare > 0:
        movable = [i for i in range(1, number_of) if holding[i] < largest] or [i for i in range(1, number_of) if holding[i] < most]
        pool, left = sum([loads[i] for i in movable]), spare
        for i in movable:
            extra = min(most - holding[i], max(1, left * loads[i] // pool), spare)
            holding[i] = holding[i] + extra
            spare = spare - extra
    return np.array(holding)


def scatter_about(own_key, dims, deviation, limit, cuts=(), kind=jnp.bfloat16):
    array = jax.random.normal(own_key, dims, jnp.float32) * deviation
    if len(cuts) > 0:
        array = level_of(own_key, dims, cuts, -0.22, 0.18) * array
    return jnp.clip(array, min=-limit, max=limit).astype(kind)


def setup_inputs(seed: int = 0) -> dict:
    seeds = jax.random.split(jax.random.key(seed), 7)
    activations = scatter_about(seeds[0], (TOKENS, D), 1.0, 6.0, ((0, 128),))
    expert_ids_keys = jax.random.split(jax.random.fold_in(seeds[1], 1), TOKENS // TOK_DEV)
    expert_ids_turns = jax.random.permutation(jax.random.fold_in(seeds[1], 3), TOKENS // TOK_DEV)
    expert_ids = jax.vmap(lambda own, number: deal_out(jax.random.fold_in(seeds[1], 2), own, number, TOK_DEV, EXPERTS, TOPK, MOST, 2))(expert_ids_keys, expert_ids_turns).reshape((TOKENS, TOPK))
    route_weights = jnp.clip(0.099609375 + 0.40039062 * jax.random.uniform(seeds[2], (TOKENS, TOPK), jnp.float32) ** level_of(seeds[2], (TOKENS, TOPK), ((0, 128),), -0.2, 0.2), 0.099609375, 0.5).astype(jnp.bfloat16)
    w_gate = scatter_about(seeds[3], (EXPERTS, D, FF), D ** -0.5, 0.0625, ((0, 16), (2, 8)))
    w_up = scatter_about(seeds[4], (EXPERTS, D, FF), D ** -0.5, 0.0625, ((0, 16), (2, 8)))
    w_down = scatter_about(seeds[5], (EXPERTS, FF, D), FF ** -0.5, 0.125, ((0, 16), (1, 8)))
    return dict(activations=activations, expert_ids=expert_ids, route_weights=route_weights, w_gate=w_gate, w_up=w_up, w_down=w_down)


def reference(activations, expert_ids, route_weights, w_gate, w_up, w_down):
    reach = MOST * N_NODE * N_LOCAL
    slice_width = FF // N_NODE
    total = jnp.zeros((TOKENS, D), jnp.float32)

    def one_expert(carry, expert):
        hits = expert_ids == expert
        chosen = jnp.any(hits, axis=1)
        row_weight = jnp.sum(jnp.where(hits, route_weights.astype(jnp.float32), 0.0), axis=1)
        index = jnp.nonzero(chosen, size=reach, fill_value=0)[0].astype(jnp.int32)
        valid = (jnp.arange(reach) < jnp.sum(chosen)).astype(jnp.float32)
        picked = activations[index]
        gate = jnp.dot(picked, w_gate[expert], preferred_element_type=jnp.float32)
        up = jnp.dot(picked, w_up[expert], preferred_element_type=jnp.float32)
        hidden = (jax.nn.silu(gate) * up).astype(jnp.bfloat16)
        sliced = hidden.astype(jnp.float32).reshape(reach, N_NODE, slice_width)
        down = w_down[expert].astype(jnp.float32).reshape(N_NODE, slice_width, D)
        part = jnp.einsum("rnf,nfd->nrd", sliced, down)
        weight = row_weight[index] * valid
        contrib = (part * weight[None, :, None]).astype(jnp.bfloat16)
        summed = jnp.sum(contrib.astype(jnp.float32), axis=0)
        return carry.at[index].add(summed * valid[:, None]), None

    total, _ = lax.scan(one_expert, total, jnp.arange(EXPERTS, dtype=jnp.int32))
    return total.astype(jnp.bfloat16)
```

```python
import jax
import jax.numpy as jnp
from jax import lax
from jax.experimental import pallas as pl
from jax.experimental.pallas import tpu as pltpu
from jax.sharding import PartitionSpec as P

MESH = pl.DeviceIdType.MESH
F32 = jnp.float32
BF16 = jnp.bfloat16

SIDE = 4
ROWS = 16
HALF = 3584
EXTRA = 128
FFS = 256
PARTS = (
    ((0, 1, 2), 0, 1280, 1280),
    ((1, 2, 0), 1280, 1280, 1280),
    ((2, 0, 1), 2560, 1024, 1152),
)


def kernel(
    x_in, ids_in, rw_in, wg_hbm, wu_hbm, wd_hbm, out_ref,
    pack, pack_got, xb0, xb1, xb2, wgu, wd, acc, hb,
    ob0, ob1, ob2, ro0, ro1, ro2, rp0, rp1, rp2, rm0, rm1, rm2,
    bo0, bo1, bo2, bp0, bp1, bp2, bm0, bm1, bm2, ra0, ra1, ra2,
    fin, fin_got, ssem, rsem, lsem,
):
    node = lax.axis_index("node")
    local = lax.axis_index("local")
    core = lax.rem(node, 2)
    me = (local // SIDE, lax.rem(local, SIDE), node // 2)
    mate = 1 - core
    xb, ob = (xb0, xb1, xb2), (ob0, ob1, ob2)
    ro, rp, rm = (ro0, ro1, ro2), (rp0, rp1, rp2), (rm0, rm1, rm2)
    bo, bp, bm, ra = (bo0, bo1, bo2), (bp0, bp1, bp2), (bm0, bm1, bm2), (ra0, ra1, ra2)

    def off(d, k):
        return lax.rem(me[d] + k, SIDE)

    def device(d=None, k=0, other_core=False):
        at = [off(i, k) if i == d else me[i] for i in range(3)]
        return (at[2] * 2 + (mate if other_core else core), at[0] * SIDE + at[1])

    def ix(*pairs):
        at = [slice(None)] * 3
        for d, v in pairs:
            at[d] = v
        return tuple(at)

    copies = []

    def send(src, dst, to):
        n = len(copies)
        cp = pltpu.make_async_remote_copy(
            src_ref=src, dst_ref=dst, send_sem=ssem.at[n], recv_sem=rsem.at[n], device_id=to, device_id_type=MESH
        )
        cp.start()
        copies.append(cp)
        return cp

    loads = []
    for e in range(2):
        for g, w in enumerate((wg_hbm, wu_hbm)):
            for h in range(2):
                n = len(loads)
                cp = pltpu.make_async_copy(w.at[e, pl.ds(h * HALF, HALF)], wgu.at[2 * e + g, h], lsem.at[n])
                cp.start()
                loads.append(cp)
    own_cols = pl.ds(pl.multiple_of(core * HALF, 128), HALF)
    mate_cols = pl.ds(pl.multiple_of(mate * HALF, 128), HALF)
    cp = pltpu.make_async_copy(wd_hbm.at[:, :, own_cols], wd.at[core], lsem.at[len(loads)])
    cp.start()
    loads.append(cp)

    barrier = pltpu.get_barrier_semaphore()
    peers = [device(other_core=True)] + [device(d, k) for d in range(3) for k in (1, 2, 3)]
    for peer in peers:
        pl.semaphore_signal(barrier, inc=1, device_id=peer, device_id_type=MESH)

    lane = lax.broadcasted_iota(jnp.int32, (8, EXTRA), 1)
    dense = jnp.zeros((8, EXTRA), F32)
    ids = ids_in[...]
    rw = rw_in[...].astype(F32)
    for k in range(8):
        dense = dense + jnp.where(ids[:, k : k + 1] == lane, rw[:, k : k + 1], 0.0)
    for h in range(2):
        pack[h, :, 0:HALF] = x_in[:, h * HALF : (h + 1) * HALF].astype(F32)
        pack[h, :, HALF : HALF + EXTRA] = dense

    pl.semaphore_wait(barrier, len(peers))
    sister = device(other_core=True)
    swap = send(pack.at[mate], pack_got, sister)
    wd_cp = send(wd_hbm.at[:, :, mate_cols], wd.at[core], sister)
    acc[...] = jnp.zeros_like(acc)
    swap.wait_recv()
    mine, got = pack[core], pack_got[...]
    first = core == 0
    block = jnp.concatenate([jnp.where(first, mine, got), jnp.where(first, got, mine)], axis=0).astype(BF16)
    for p, (_, c0, _, width) in enumerate(PARTS):
        xb[p][core, me[0], me[1], me[2]] = block[:, c0 : c0 + width]

    def gather(p, at, to):
        ref = xb[p].at[(core,) + at]
        return send(ref, ref, to)

    first_hop = []
    for p, ((a, b, c), *_) in enumerate(PARTS):
        at = ix((a, me[a]), (b, me[b]), (c, me[c]))
        first_hop.append([gather(p, at, device(a, k)) for k in (1, 3, 2)])
    line, plane_own, mate_parts = [], [], []
    for p, ((a, b, c), *_) in enumerate(PARTS):
        for cp in first_hop[p]:
            cp.wait_recv()
        at = ix((b, me[b]), (c, me[c]))
        line.append([gather(p, at, device(b, k)) for k in (1, 3)])
        plane_own.append([gather(p, at, device(c, k)) for k in (1, 3)])
        mate_parts.append([gather(p, at, sister)])
    line_far, plane_side = [], []
    for p, ((a, b, c), *_) in enumerate(PARTS):
        up, down = line[p]
        up.wait_recv()
        far = [gather(p, ix((a, pl.ds(0, 2)), (b, off(b, 3)), (c, me[c])), device(b, 1))]
        down.wait_recv()
        far.append(gather(p, ix((a, pl.ds(2, 2)), (b, off(b, 1)), (c, me[c])), device(b, 3)))
        line_far.append(far)
        side = []
        for k in (1, 3):
            at = ix((b, off(b, k)), (c, me[c]))
            side.append([gather(p, at, device(c, j)) for j in (1, 3)])
            mate_parts[p].append(gather(p, at, sister))
        plane_side.append(side)
    plane_far = []
    for p, ((a, b, c), *_) in enumerate(PARTS):
        for cp in line_far[p]:
            cp.wait_recv()
        at = ix((b, off(b, 2)), (c, me[c]))
        plane_far.append([gather(p, at, device(c, j)) for j in (1, 3)])
        mate_parts[p].append(gather(p, at, sister))

    def gate_up(p, h, ci):
        (_, _, c), c0, cols, _ = PARTS[p]
        at = ix((c, ci))

        def one(m, carry):
            x = xb[p][(h,) + at + (slice(None), slice(0, cols))].reshape(256, cols)
            w = wgu[m, h, c0 : c0 + cols]
            r = jnp.dot(x, w, preferred_element_type=F32)
            acc[(m,) + at] += r.reshape(SIDE, SIDE, ROWS, FFS)
            return carry

        lax.fori_loop(0, 4, one, 0)

    opposite = [[] for _ in PARTS]
    for p, ((a, b, c), *_) in enumerate(PARTS):
        up, down = plane_own[p]
        up.wait_recv()
        opposite[p].append(gather(p, ix((b, me[b]), (c, off(c, 3))), device(c, 1)))
        down.wait_recv()
    for cp in loads:
        cp.wait()
    for p, ((a, b, c), *_) in enumerate(PARTS):
        gate_up(p, core, me[c])
    for p, ((a, b, c), *_) in enumerate(PARTS):
        for k, (up, down) in zip((1, 3), plane_side[p]):
            up.wait_recv()
            down.wait_recv()
            if k == 1:
                opposite[p].append(gather(p, ix((b, off(b, 1)), (c, off(c, 3))), device(c, 1)))
            else:
                opposite[p].append(gather(p, ix((b, off(b, 3)), (c, off(c, 1))), device(c, 3)))
    for p, ((a, b, c), *_) in enumerate(PARTS):
        for cp in mate_parts[p]:
            cp.wait_recv()
        gate_up(p, mate, me[c])
    mate_side = [[] for _ in PARTS]
    for p, ((a, b, c), *_) in enumerate(PARTS):
        up, down = plane_far[p]
        down.wait_recv()
        opposite[p].append(gather(p, ix((b, off(b, 2)), (c, off(c, 1))), device(c, 3)))
        up.wait_recv()
        for k in (1, 3):
            mate_side[p].append(gather(p, ix((c, off(c, k))), sister))
    for p, ((a, b, c), *_) in enumerate(PARTS):
        for k in (1, 3):
            gate_up(p, core, off(c, k))
    for p, ((a, b, c), *_) in enumerate(PARTS):
        for k, cp in zip((1, 3), mate_side[p]):
            cp.wait_recv()
            gate_up(p, mate, off(c, k))
    mate_far = []
    for p, ((a, b, c), *_) in enumerate(PARTS):
        for cp in opposite[p]:
            cp.wait_recv()
        mate_far.append(gather(p, ix((c, off(c, 2))), sister))
    for p, ((a, b, c), *_) in enumerate(PARTS):
        gate_up(p, core, off(c, 2))
    for p, ((a, b, c), *_) in enumerate(PARTS):
        mate_far[p].wait_recv()
        gate_up(p, mate, off(c, 2))

    expert = lax.broadcasted_iota(jnp.int32, (256, EXTRA), 1) - local * 2
    hidden_cp = []
    for i in range(SIDE):
        dense = xb2[core, i, :, :, :, 1024:1152].reshape(256, EXTRA).astype(F32)
        for e in range(2):
            weight = jnp.sum(jnp.where(expert == e, dense, 0.0), axis=1, keepdims=True)
            gate = acc[2 * e, i].reshape(256, FFS)
            up = acc[2 * e + 1, i].reshape(256, FFS)
            hidden = gate / (1.0 + jnp.exp(-gate)) * up * weight
            hb[core, i, :, :, :, e * FFS : (e + 1) * FFS] = hidden.astype(BF16).reshape(SIDE, SIDE, ROWS, FFS)
        hidden_cp.append(send(hb.at[core, i], hb.at[core, i], sister))
    wd_cp.wait_recv()
    for cp in hidden_cp:
        cp.wait_recv()

    def project(p, ci):
        (_, _, c), c0, cols, _ = PARTS[p]
        at = ix((c, ci))

        def one(n, carry):
            h0 = hb[(0,) + at].reshape(256, 2 * FFS)
            h1 = hb[(1,) + at].reshape(256, 2 * FFS)
            h = jnp.concatenate([h0, h1], axis=1)
            w = wd[:, :, :, pl.ds(pl.multiple_of(c0 + n * 256, 256), 256)].reshape(4 * FFS, 256)
            r = jnp.dot(h, w, preferred_element_type=F32).astype(BF16)
            ob[p][at + (slice(None), pl.ds(pl.multiple_of(n * 256, 256), 256))] = r.reshape(SIDE, SIDE, ROWS, 256)
            return carry

        lax.fori_loop(0, cols // 256, one, 0)

    def add(dst, dst_at, *others):
        total = dst[dst_at].astype(F32)
        for ref, at in others:
            total = total + ref[at].astype(F32)
        dst[dst_at] = total.astype(BF16)

    far_cp, side_cp = [], [[None] * 8 for _ in PARTS]
    for p, ((a, b, c), *_) in enumerate(PARTS):
        project(p, off(c, 2))
        cps = []
        for k in (2, 1, 3, 0):
            to = 1 if k in (2, 1) else 3
            at = ix((b, off(b, k)), (c, off(c, 2)))
            cps.append(send(ob[p].at[at], ro[p].at[off(b, k)], device(c, to)))
        far_cp.append(cps)
    for p, ((a, b, c), *_) in enumerate(PARTS):
        for s, into in ((1, rp), (3, rm)):
            project(p, off(c, s))
            for k in (3, 0) if s == 1 else (2, 1):
                at = ix((b, off(b, k)), (c, off(c, s)))
                side_cp[p][(0 if s == 1 else 4) + k] = send(ob[p].at[at], into[p].at[off(b, k)], device(c, s))
    for p, ((a, b, c), *_) in enumerate(PARTS):
        project(p, me[c])
    for pair in range(2):
        for p, ((a, b, c), *_) in enumerate(PARTS):
            for s, into in ((1, rp), (3, rm)):
                k = ((2, 1) if s == 1 else (3, 0))[pair]
                far_cp[p][(2, 1, 3, 0).index(k)].wait_recv()
                at = ix((b, off(b, k)), (c, off(c, s)))
                add(ob[p], at, (ro[p], off(b, k)))
                side_cp[p][(0 if s == 1 else 4) + k] = send(ob[p].at[at], into[p].at[off(b, k)], device(c, s))
    low, high = pl.ds(0, 2), pl.ds(2, 2)
    line_opp, line_cp = [None] * 3, [[] for _ in PARTS]
    for k in (2, 3, 1, 0):
        for p, ((a, b, c), *_) in enumerate(PARTS):
            side_cp[p][k].wait_recv()
            side_cp[p][4 + k].wait_recv()
            add(ob[p], ix((b, off(b, k)), (c, me[c])), (rp[p], off(b, k)), (rm[p], off(b, k)))

            def part_of(h, k=k, a=a, b=b, c=c):
                return ix((a, h), (b, off(b, k)), (c, me[c]))

            if k == 2:
                line_opp[p] = (
                    send(ob[p].at[part_of(low)], bo[p].at[low], device(b, 1)),
                    send(ob[p].at[part_of(high)], bo[p].at[high], device(b, 3)),
                )
            elif k == 1:
                line_cp[p].append(send(ob[p].at[part_of(high)], bp[p].at[high], device(b, 1)))
                line_opp[p][0].wait_recv()
                add(ob[p], part_of(low), (bo[p], low))
                line_cp[p].append(send(ob[p].at[part_of(low)], bp[p].at[low], device(b, 1)))
            elif k == 3:
                line_cp[p].append(send(ob[p].at[part_of(low)], bm[p].at[low], device(b, 3)))
                line_opp[p][1].wait_recv()
                add(ob[p], part_of(high), (bo[p], high))
                line_cp[p].append(send(ob[p].at[part_of(high)], bm[p].at[high], device(b, 3)))
    last = [[] for _ in PARTS]
    for p, ((a, b, c), *_) in enumerate(PARTS):
        for cp in line_cp[p]:
            cp.wait_recv()
        add(ob[p], ix((b, me[b]), (c, me[c])), (bp[p], slice(None)), (bm[p], slice(None)))
        for k in (1, 2, 3):
            at = ix((a, off(a, k)), (b, me[b]), (c, me[c]))
            last[p].append(send(ob[p].at[at], ra[p].at[k - 1], device(a, k)))
    for p, ((a, b, c), c0, cols, _) in enumerate(PARTS):
        total = ob[p][me].astype(F32)
        for k in (1, 2, 3):
            last[p][k - 1].wait_recv()
            total = total + ra[p][k - 1].astype(F32)
        fin[0, :, c0 : c0 + cols] = total[0:8]
        fin[1, :, c0 : c0 + cols] = total[8:16]
    final = send(fin.at[mate], fin_got, sister)
    final.wait_recv()
    mine, got = fin[core], fin_got[...]
    out_ref[:, 0:HALF] = jnp.where(first, mine, got).astype(BF16)
    out_ref[:, HALF : 2 * HALF] = jnp.where(first, got, mine).astype(BF16)
    for cp in copies:
        cp.wait_send()


N_COPIES = 170


def body(activations, expert_ids, route_weights, w_gate, w_up, w_down):
    rows, width = activations.shape
    sums = [p[2] for p in PARTS]
    sent = [p[3] for p in PARTS]
    vmem = pltpu.VMEM
    scratch = (
        [vmem((2, 8, HALF + EXTRA), F32), vmem((8, HALF + EXTRA), F32)]
        + [vmem((2, SIDE, SIDE, SIDE, ROWS, w), BF16) for w in sent]
        + [
            vmem((4, 2, HALF, FFS), BF16),
            vmem((2, 2, FFS, HALF), BF16),
            vmem((4, SIDE, SIDE, SIDE, ROWS, FFS), F32),
            vmem((2, SIDE, SIDE, SIDE, ROWS, 2 * FFS), BF16),
        ]
        + [vmem((SIDE, SIDE, SIDE, ROWS, w), BF16) for w in sums]
        + [vmem((SIDE, SIDE, ROWS, w), BF16) for _ in range(3) for w in sums]
        + [vmem((SIDE, ROWS, w), BF16) for _ in range(3) for w in sums]
        + [vmem((3, ROWS, w), BF16) for w in sums]
        + [vmem((2, 8, HALF), F32), vmem((8, HALF), F32)]
        + [pltpu.SemaphoreType.DMA((N_COPIES,)), pltpu.SemaphoreType.DMA((N_COPIES,)), pltpu.SemaphoreType.DMA((9,))]
    )
    in_vmem = pl.BlockSpec(memory_space=pltpu.VMEM)
    in_hbm = pl.BlockSpec(memory_space=pl.ANY)
    return pl.pallas_call(
        kernel,
        out_shape=jax.ShapeDtypeStruct((rows, width), BF16),
        in_specs=[in_vmem] * 3 + [in_hbm] * 3,
        out_specs=in_vmem,
        scratch_shapes=scratch,
        compiler_params=pltpu.CompilerParams(
            collective_id=0, has_side_effects=True, vmem_limit_bytes=62 * 2**20
        ),
        cost_estimate=pl.CostEstimate(flops=2 * 1024 * 7168 * 1536, bytes_accessed=22 * 2**20, transcendentals=2**19),
    )(activations, expert_ids, route_weights, w_gate, w_up, w_down)


def solution(mesh):
    return jax.shard_map(
        body,
        mesh=mesh,
        in_specs=(
            P(("node", "local"), None),
            P(("node", "local"), None),
            P(("node", "local"), None),
            P("local", None, "node"),
            P("local", None, "node"),
            P("local", "node", None),
        ),
        out_specs=P(("node", "local"), None),
        check_vma=False,
    )
```

```python
import jax
import jax.numpy as jnp
from jax import lax
from jax.experimental import pallas as pl
from jax.experimental.pallas import tpu as pltpu
from jax.sharding import PartitionSpec as P

MESH = pl.DeviceIdType.MESH
F32 = jnp.float32
BF16 = jnp.bfloat16

SIDE = 4
ROWS = 16
HALF = 3584
EXTRA = 128
FFS = 256
PARTS = (
    ((0, 1, 2), 0, 1280, 1280),
    ((1, 2, 0), 1280, 1280, 1280),
    ((2, 0, 1), 2560, 1024, 1152),
)


def kernel(
    x_in, ids_in, rw_in, wg_hbm, wu_hbm, wd_hbm, out_ref,
    pack, pair, xb0, xb1, xb2, wgu, wd, acc, hb,
    ob0, ob1, ob2, ro0, ro1, ro2, rp0, rp1, rp2, rm0, rm1, rm2,
    bo0, bo1, bo2, bp0, bp1, bp2, bm0, bm1, bm2, ra0, ra1, ra2,
    fin, fin_got, ssem, rsem, lsem,
):
    node = lax.axis_index("node")
    local = lax.axis_index("local")
    core = lax.rem(node, 2)
    me = (local // SIDE, lax.rem(local, SIDE), node // 2)
    mate = 1 - core
    xb, ob = (xb0, xb1, xb2), (ob0, ob1, ob2)
    ro, rp, rm = (ro0, ro1, ro2), (rp0, rp1, rp2), (rm0, rm1, rm2)
    bo, bp, bm, ra = (bo0, bo1, bo2), (bp0, bp1, bp2), (bm0, bm1, bm2), (ra0, ra1, ra2)

    def off(d, k):
        return lax.rem(me[d] + k, SIDE)

    def device(d=None, k=0, other_core=False):
        at = [off(i, k) if i == d else me[i] for i in range(3)]
        return (at[2] * 2 + (mate if other_core else core), at[0] * SIDE + at[1])

    def ix(*pairs):
        at = [slice(None)] * 3
        for d, v in pairs:
            at[d] = v
        return tuple(at)

    copies, drained = [], []

    def drain(cps):
        for cp in cps:
            cp.wait_send()
            drained.append(cp)

    def send(src, dst, to):
        n = len(copies)
        cp = pltpu.make_async_remote_copy(
            src_ref=src, dst_ref=dst, send_sem=ssem.at[n], recv_sem=rsem.at[n], device_id=to, device_id_type=MESH
        )
        cp.start()
        copies.append(cp)
        return cp

    barrier = pltpu.get_barrier_semaphore()
    peers = [device(other_core=True)] + [device(d, k) for d in range(3) for k in (1, 2, 3)]
    for peer in peers:
        pl.semaphore_signal(barrier, inc=1, device_id=peer, device_id_type=MESH)

    lane = lax.broadcasted_iota(jnp.int32, (8, EXTRA), 1)
    dense = jnp.zeros((8, EXTRA), F32)
    ids = ids_in[...]
    rw = rw_in[...].astype(F32)
    for k in range(8):
        dense = dense + jnp.where(ids[:, k : k + 1] == lane, rw[:, k : k + 1], 0.0)
    pack[0, :, 0:HALF] = x_in[:, pl.ds(pl.multiple_of(mate * HALF, 128), HALF)].astype(F32)
    pack[0, :, HALF : HALF + EXTRA] = dense
    pair[core, :, 0:HALF] = x_in[:, pl.ds(pl.multiple_of(core * HALF, 128), HALF)].astype(F32)
    pair[core, :, HALF : HALF + EXTRA] = dense

    pl.semaphore_wait(barrier, len(peers))
    sister = device(other_core=True)
    swap = send(pack.at[0], pair.at[core], sister)
    swap.wait_recv()
    for p, (_, c0, _, width) in enumerate(PARTS):
        block = pair[:, :, c0 : c0 + width].reshape(ROWS, width)
        xb[p][core, me[0], me[1], me[2]] = block.astype(BF16)

    def gather(p, at, to):
        ref = xb[p].at[(core,) + at]
        return send(ref, ref, to)

    first_hop = []
    for p, ((a, b, c), *_) in enumerate(PARTS):
        at = ix((a, me[a]), (b, me[b]), (c, me[c]))
        first_hop.append([gather(p, at, device(a, k)) for k in (1, 3, 2)])

    loads = []
    for e in range(2):
        for g, w in enumerate((wg_hbm, wu_hbm)):
            for h in range(2):
                n = len(loads)
                cp = pltpu.make_async_copy(w.at[e, pl.ds(h * HALF, HALF)], wgu.at[2 * e + g, h], lsem.at[n])
                cp.start()
                loads.append(cp)
    own_cols = pl.ds(pl.multiple_of(core * HALF, 128), HALF)
    mate_cols = pl.ds(pl.multiple_of(mate * HALF, 128), HALF)
    cp = pltpu.make_async_copy(wd_hbm.at[:, :, own_cols], wd.at[core], lsem.at[len(loads)])
    cp.start()
    loads.append(cp)

    wd_cp = send(wd_hbm.at[:, :, mate_cols], wd.at[core], sister)
    acc[...] = jnp.zeros_like(acc)

    low, high = pl.ds(0, 2), pl.ds(2, 2)
    near_got = [[None] * 4 for _ in PARTS]
    far_got = [[None] * 4 for _ in PARTS]
    mate_got = [[[] for _ in range(5)] for _ in PARTS]

    def spread(p, k):
        (a, b, c), *_ = PARTS[p]
        at = ix((b, off(b, k)), (c, me[c]))
        near_got[p][k] = [gather(p, at, device(c, j)) for j in (1, 3)]

    def pass_on(p, k):
        (a, b, c), *_ = PARTS[p]
        bi = off(b, k)
        cps = []
        for cp, half, j, to in zip(near_got[p][k], (low, high), (3, 1), (1, 3)):
            cp.wait_recv()
            cps.append(gather(p, ix((a, half), (b, bi), (c, off(c, j))), device(c, to)))
            mate_got[p][k].append(gather(p, ix((b, bi), (c, off(c, j))), sister))
        far_got[p][k] = cps

    def far_to_mate(p, k):
        (a, b, c), *_ = PARTS[p]
        for cp in far_got[p][k]:
            cp.wait_recv()
        mate_got[p][k].append(gather(p, ix((b, off(b, k)), (c, off(c, 2))), sister))

    def gate_up(p, h, k):
        (_, b, c), c0, cols, _ = PARTS[p]
        if k == 4:
            lines = [ix((b, i), (c, me[c])) for i in range(SIDE)]
        else:
            lines = [ix((b, off(b, k)), (c, off(c, j))) for j in (1, 3, 2)]
        n = SIDE * ROWS
        x = jnp.concatenate([xb[p][(h,) + at + (slice(None), slice(0, cols))].reshape(n, cols) for at in lines], axis=0)
        for m in range(4):
            r = jnp.dot(x, wgu[m, h, c0 : c0 + cols], preferred_element_type=F32)
            for i, at in enumerate(lines):
                acc[(m,) + at] += r[i * n : (i + 1) * n].reshape(SIDE, ROWS, FFS)

    def own(k):
        for p in range(3):
            gate_up(p, core, k)

    def other(k):
        for p in range(3):
            for cp in mate_got[p][k]:
                cp.wait_recv()
            gate_up(p, mate, k)

    line, line_far = [], []
    for p, ((a, b, c), *_) in enumerate(PARTS):
        for cp in first_hop[p]:
            cp.wait_recv()
        at = ix((b, me[b]), (c, me[c]))
        line.append([gather(p, at, device(b, k)) for k in (1, 3)])
    for p in range(3):
        drain(line[p])
        spread(p, 0)
    for p, ((a, b, c), *_) in enumerate(PARTS):
        up, down = line[p]
        up.wait_recv()
        cps = [gather(p, ix((a, low), (b, off(b, 3)), (c, me[c])), device(b, 1))]
        down.wait_recv()
        cps.append(gather(p, ix((a, high), (b, off(b, 1)), (c, me[c])), device(b, 3)))
        line_far.append(cps)
        spread(p, 1)
    for p in range(3):
        pass_on(p, 0)
    for p, ((a, b, c), *_) in enumerate(PARTS):
        for cp in line_far[p]:
            cp.wait_recv()
        spread(p, 3)
        mate_got[p][4].append(gather(p, ix((c, me[c])), sister))
    for cp in loads:
        cp.wait()
    own(4)
    for p in range(3):
        pass_on(p, 1)
        spread(p, 2)
    other(4)
    for k, later in ((0, 3), (1, 2), (3, None), (2, None)):
        for p in range(3):
            far_to_mate(p, k)
        own(k)
        if later is not None:
            for p in range(3):
                pass_on(p, later)
        other(k)

    expert = lax.broadcasted_iota(jnp.int32, (256, EXTRA), 1) - local * 2
    hidden_cp = []
    for k in (2, 1, 3, 0):
        i = off(0, k)
        dense = xb2[core, i, :, :, :, 1024:1152].reshape(256, EXTRA).astype(F32)
        for e in range(2):
            weight = jnp.sum(jnp.where(expert == e, dense, 0.0), axis=1, keepdims=True)
            gate = acc[2 * e, i].reshape(256, FFS)
            up = acc[2 * e + 1, i].reshape(256, FFS)
            hidden = gate / (1.0 + jnp.exp(-gate)) * up * weight
            hb[core, i, :, :, :, e * FFS : (e + 1) * FFS] = hidden.astype(BF16).reshape(SIDE, SIDE, ROWS, FFS)
        hidden_cp.append(send(hb.at[core, i], hb.at[core, i], sister))
    wd_cp.wait_recv()

    def project(p, k):
        (_, b, _), c0, cols, _ = PARTS[p]
        at = ix((b, off(b, k)))

        h = jnp.concatenate([hb[(core_of,) + at].reshape(256, 2 * FFS) for core_of in range(2)], axis=1)
        for n in range(cols // 256):
            w = wd[:, :, :, c0 + n * 256 : c0 + (n + 1) * 256].reshape(4 * FFS, 256)
            r = jnp.dot(h, w, preferred_element_type=F32).astype(BF16)
            ob[p][at + (slice(None), slice(n * 256, (n + 1) * 256))] = r.reshape(SIDE, SIDE, ROWS, 256)

    def add(dst, dst_at, *others):
        total = dst[dst_at].astype(F32)
        for ref, at in others:
            total = total + ref[at].astype(F32)
        dst[dst_at] = total.astype(BF16)

    far_cp = [[None] * 4 for _ in PARTS]
    side_cp = [[[] for _ in range(4)] for _ in PARTS]

    def begin(p, k):
        (a, b, c), *_ = PARTS[p]
        project(p, k)
        bi = off(b, k)

        def to(half, s, into, j):
            return send(ob[p].at[ix((a, half), (b, bi), (c, off(c, s)))], into[p].at[bi, half], device(c, j))

        far_cp[p][k] = (to(low, 2, ro, 1), to(high, 2, ro, 3))
        side_cp[p][k] += [to(high, 1, rp, 1), to(low, 3, rm, 3)]

    def relay(p, k):
        (a, b, c), *_ = PARTS[p]
        bi = off(b, k)
        for cp, half, s, into in zip(far_cp[p][k], (low, high), (1, 3), (rp, rm)):
            cp.wait_recv()
            at = ix((a, half), (b, bi), (c, off(c, s)))
            add(ob[p], at, (ro[p], (bi, half)))
            side_cp[p][k].append(send(ob[p].at[at], into[p].at[bi, half], device(c, s)))

    def settle(p, k):
        (a, b, c), *_ = PARTS[p]
        bi = off(b, k)
        for cp in side_cp[p][k]:
            cp.wait_recv()
        add(ob[p], ix((b, bi), (c, me[c])), (rp[p], bi), (rm[p], bi))

    line_opp, line_cp = [None] * 3, [[] for _ in PARTS]

    def along_b(p, k, half, into, j):
        (a, b, c), *_ = PARTS[p]
        return send(ob[p].at[ix((a, half), (b, off(b, k)), (c, me[c]))], into[p].at[half], device(b, j))

    hidden_cp[0].wait_recv()
    begin(2, 2)
    for cp in hidden_cp[1:]:
        cp.wait_recv()
    for p in (0, 1):
        begin(p, 2)
    for p in (2, 0, 1):
        begin(p, 1)
    for p in (2, 0, 1):
        relay(p, 2)
        begin(p, 3)
    for p in (2, 0, 1):
        relay(p, 1)
        begin(p, 0)
    for p in (2, 0, 1):
        settle(p, 2)
        line_opp[p] = (along_b(p, 2, low, bo, 1), along_b(p, 2, high, bo, 3))
        relay(p, 3)
    for p in (2, 0, 1):
        relay(p, 0)
        settle(p, 1)
        line_cp[p].append(along_b(p, 1, high, bp, 1))
    for p in (2, 0, 1):
        settle(p, 3)
        line_cp[p].append(along_b(p, 3, low, bm, 3))
    for p, ((a, b, c), *_) in enumerate(PARTS):
        line_opp[p][0].wait_recv()
        add(ob[p], ix((a, low), (b, off(b, 1)), (c, me[c])), (bo[p], low))
        line_cp[p].append(along_b(p, 1, low, bp, 1))
        line_opp[p][1].wait_recv()
        add(ob[p], ix((a, high), (b, off(b, 3)), (c, me[c])), (bo[p], high))
        line_cp[p].append(along_b(p, 3, high, bm, 3))
    last = [[] for _ in PARTS]
    for p, ((a, b, c), *_) in enumerate(PARTS):
        settle(p, 0)
        for cp in line_cp[p]:
            cp.wait_recv()
        add(ob[p], ix((b, me[b]), (c, me[c])), (bp[p], slice(None)), (bm[p], slice(None)))
        for k in (1, 2, 3):
            at = ix((a, off(a, k)), (b, me[b]), (c, me[c]))
            last[p].append(send(ob[p].at[at], ra[p].at[k - 1], device(a, k)))
    for p, ((a, b, c), c0, cols, _) in enumerate(PARTS):
        total = ob[p][me].astype(F32)
        for k in (1, 2, 3):
            last[p][k - 1].wait_recv()
            total = total + ra[p][k - 1].astype(F32)
        fin[0, :, c0 : c0 + cols] = total[0:8]
        fin[1, :, c0 : c0 + cols] = total[8:16]
    final = send(fin.at[mate], fin_got, sister)
    final.wait_recv()
    first = core == 0
    mine, got = fin[core], fin_got[...]
    out_ref[:, 0:HALF] = jnp.where(first, mine, got).astype(BF16)
    out_ref[:, HALF : 2 * HALF] = jnp.where(first, got, mine).astype(BF16)
    for cp in copies:
        if not any(cp is other for other in drained):
            cp.wait_send()
    assert len(copies) == N_COPIES


N_COPIES = 214


def body(activations, expert_ids, route_weights, w_gate, w_up, w_down):
    rows, width = activations.shape
    sums = [p[2] for p in PARTS]
    sent = [p[3] for p in PARTS]
    vmem = pltpu.VMEM
    scratch = (
        [vmem((1, 8, HALF + EXTRA), F32), vmem((2, 8, HALF + EXTRA), F32)]
        + [vmem((2, SIDE, SIDE, SIDE, ROWS, w), BF16) for w in sent]
        + [
            vmem((4, 2, HALF, FFS), BF16),
            vmem((2, 2, FFS, HALF), BF16),
            vmem((4, SIDE, SIDE, SIDE, ROWS, FFS), F32),
            vmem((2, SIDE, SIDE, SIDE, ROWS, 2 * FFS), BF16),
        ]
        + [vmem((SIDE, SIDE, SIDE, ROWS, w), BF16) for w in sums]
        + [vmem((SIDE, SIDE, ROWS, w), BF16) for _ in range(3) for w in sums]
        + [vmem((SIDE, ROWS, w), BF16) for _ in range(3) for w in sums]
        + [vmem((3, ROWS, w), BF16) for w in sums]
        + [vmem((2, 8, HALF), F32), vmem((8, HALF), F32)]
        + [pltpu.SemaphoreType.DMA((N_COPIES,)), pltpu.SemaphoreType.DMA((N_COPIES,)), pltpu.SemaphoreType.DMA((9,))]
    )
    in_vmem = pl.BlockSpec(memory_space=pltpu.VMEM)
    in_hbm = pl.BlockSpec(memory_space=pl.ANY)
    return pl.pallas_call(
        kernel,
        out_shape=jax.ShapeDtypeStruct((rows, width), BF16),
        in_specs=[in_vmem] * 3 + [in_hbm] * 3,
        out_specs=in_vmem,
        scratch_shapes=scratch,
        compiler_params=pltpu.CompilerParams(
            collective_id=0, has_side_effects=True, vmem_limit_bytes=62 * 2**20
        ),
        cost_estimate=pl.CostEstimate(flops=2 * 1024 * 7168 * 1536, bytes_accessed=22 * 2**20, transcendentals=2**19),
    )(activations, expert_ids, route_weights, w_gate, w_up, w_down)


def solution(mesh):
    return jax.shard_map(
        body,
        mesh=mesh,
        in_specs=(
            P(("node", "local"), None),
            P(("node", "local"), None),
            P(("node", "local"), None),
            P("local", None, "node"),
            P("local", None, "node"),
            P("local", "node", None),
        ),
        out_specs=P(("node", "local"), None),
        check_vma=False,
    )
```

```python
import jax
import jax.numpy as jnp
from jax import lax
from jax.experimental import pallas as pl
from jax.experimental.pallas import tpu as pltpu
from jax.sharding import PartitionSpec as P

MESH = pl.DeviceIdType.MESH
F32 = jnp.float32
BF16 = jnp.bfloat16

SIDE = 4
ROWS = 16
HALF = 3584
EXTRA = 128
FFS = 256
PARTS = (
    ((0, 1, 2), 0, 1280, 1280),
    ((1, 2, 0), 2560, 1024, 1152),
    ((2, 0, 1), 1280, 1280, 1280),
)
ORDER = (0, 2, 1)


def kernel(
    x_hbm, ids_hbm, rw_hbm, wg_hbm, wu_hbm, wd_hbm, out_ref,
    x_in, ids_in, rw_in, pack, pair, xb0, xb1, xb2, wgu, wd, acc, hb,
    ob0, ob1, ob2, ro0, ro1, ro2, rp0, rp1, rp2, rm0, rm1, rm2,
    bo0, bo1, bo2, bp0, bp1, bp2, bm0, bm1, bm2, ra0, ra1, ra2,
    fin, fin_got, ssem, rsem, lsem, isem,
):
    node = lax.axis_index("node")
    local = lax.axis_index("local")
    core = lax.rem(node, 2)
    me = (local // SIDE, lax.rem(local, SIDE), node // 2)
    mate = 1 - core
    xb, ob = (xb0, xb1, xb2), (ob0, ob1, ob2)
    ro, rp, rm = (ro0, ro1, ro2), (rp0, rp1, rp2), (rm0, rm1, rm2)
    bo, bp, bm, ra = (bo0, bo1, bo2), (bp0, bp1, bp2), (bm0, bm1, bm2), (ra0, ra1, ra2)

    def off(d, k):
        return lax.rem(me[d] + k, SIDE)

    def device(d=None, k=0, other_core=False):
        at = [off(i, k) if i == d else me[i] for i in range(3)]
        return (at[2] * 2 + (mate if other_core else core), at[0] * SIDE + at[1])

    def ix(*pairs):
        at = [slice(None)] * 3
        for d, v in pairs:
            at[d] = v
        return tuple(at)

    copies, drained = [], []

    def drain(cps):
        for cp in cps:
            cp.wait_send()
            drained.append(cp)

    def send(src, dst, to):
        n = len(copies)
        cp = pltpu.make_async_remote_copy(
            src_ref=src, dst_ref=dst, send_sem=ssem.at[n], recv_sem=rsem.at[n], device_id=to, device_id_type=MESH
        )
        cp.start()
        copies.append(cp)
        return cp

    barrier = pltpu.get_barrier_semaphore()
    peers = [device(other_core=True)] + [device(d, k) for d in range(3) for k in (1, 2, 3)]
    for peer in peers:
        pl.semaphore_signal(barrier, inc=1, device_id=peer, device_id_type=MESH)

    fetches = []
    for n, (src, dst) in enumerate(((x_hbm, x_in), (ids_hbm, ids_in), (rw_hbm, rw_in))):
        fetches.append(pltpu.make_async_copy(src, dst, isem.at[n]))
        fetches[n].start()
    for cp in fetches:
        cp.wait()
    lane = lax.broadcasted_iota(jnp.int32, (8, EXTRA), 1)
    dense = jnp.zeros((8, EXTRA), F32)
    ids = ids_in[...]
    rw = rw_in[...].astype(F32)
    for k in range(8):
        dense = dense + jnp.where(ids[:, k : k + 1] == lane, rw[:, k : k + 1], 0.0)
    pack[0, :, 0:HALF] = x_in[:, pl.ds(pl.multiple_of(mate * HALF, 128), HALF)].astype(F32)
    pack[0, :, HALF : HALF + EXTRA] = dense
    pair[core, :, 0:HALF] = x_in[:, pl.ds(pl.multiple_of(core * HALF, 128), HALF)].astype(F32)
    pair[core, :, HALF : HALF + EXTRA] = dense

    pl.semaphore_wait(barrier, len(peers))
    sister = device(other_core=True)
    swap = send(pack.at[0], pair.at[core], sister)
    swap.wait_recv()
    for p, (_, c0, _, width) in enumerate(PARTS):
        block = pair[:, :, c0 : c0 + width].reshape(ROWS, width)
        xb[p][core, me[0], me[1], me[2]] = block.astype(BF16)

    def gather(p, at, to):
        ref = xb[p].at[(core,) + at]
        return send(ref, ref, to)

    first_hop = [None] * 3
    for p in ORDER:
        (a, b, c), *_ = PARTS[p]
        at = ix((a, me[a]), (b, me[b]), (c, me[c]))
        first_hop[p] = [gather(p, at, device(a, k)) for k in (2, 1, 3)]
    line, line_far = [None] * 3, [None] * 3
    near_got = [[None] * 4 for _ in PARTS]
    for p in ORDER:
        (a, b, c), *_ = PARTS[p]
        at = ix((a, me[a]), (b, me[b]), (c, me[c]))
        line[p] = [[gather(p, at, device(b, k))] for k in (1, 3)]
    for p in ORDER:
        (a, b, c), *_ = PARTS[p]
        at = ix((a, me[a]), (b, me[b]), (c, me[c]))
        near_got[p][0] = [[gather(p, at, device(c, k))] for k in (1, 3)]

    loads = []
    for e in range(2):
        for g, w in enumerate((wg_hbm, wu_hbm)):
            for h in range(2):
                n = len(loads)
                cp = pltpu.make_async_copy(w.at[e, pl.ds(h * HALF, HALF)], wgu.at[2 * e + g, h], lsem.at[n])
                cp.start()
                loads.append(cp)
    own_cols = pl.ds(pl.multiple_of(core * HALF, 128), HALF)
    mate_cols = pl.ds(pl.multiple_of(mate * HALF, 128), HALF)
    cp = pltpu.make_async_copy(wd_hbm.at[:, :, own_cols], wd.at[core], lsem.at[len(loads)])
    cp.start()
    loads.append(cp)

    wd_cp = send(wd_hbm.at[:, :, mate_cols], wd.at[core], sister)
    acc[...] = jnp.zeros_like(acc)

    low, high = pl.ds(0, 2), pl.ds(2, 2)
    far_got = [[None] * 4 for _ in PARTS]
    mate_got = [[[] for _ in range(5)] for _ in PARTS]

    def spread(p, k):
        (a, b, c), *_ = PARTS[p]
        at = ix((b, off(b, k)), (c, me[c]))
        near_got[p][k] = [[gather(p, at, device(c, j))] for j in (1, 3)]

    def pass_on(p, k):
        (a, b, c), *_ = PARTS[p]
        bi = off(b, k)
        cps = []
        for got, half, j, to in zip(near_got[p][k], (low, high), (3, 1), (1, 3)):
            for cp in got:
                cp.wait_recv()
            cps.append(gather(p, ix((a, half), (b, bi), (c, off(c, j))), device(c, to)))
            mate_got[p][k].append(gather(p, ix((b, bi), (c, off(c, j))), sister))
        far_got[p][k] = cps

    def far_to_mate(p, k):
        (a, b, c), *_ = PARTS[p]
        for cp in far_got[p][k]:
            cp.wait_recv()
        mate_got[p][k].append(gather(p, ix((b, off(b, k)), (c, off(c, 2))), sister))

    def gate_up(p, h, group):
        (_, b, c), c0, cols, _ = PARTS[p]
        lines = [ix((b, off(b, kb)), (c, off(c, kc))) for kb, kc in group]
        n = SIDE * ROWS
        x = jnp.concatenate([xb[p][(h,) + at + (slice(None), slice(0, cols))].reshape(n, cols) for at in lines], axis=0)
        for m in range(4):
            r = jnp.dot(x, wgu[m, h, c0 : c0 + cols], preferred_element_type=F32)
            for i, at in enumerate(lines):
                acc[(m,) + at] += r[i * n : (i + 1) * n].reshape(SIDE, ROWS, FFS)

    def own(group):
        for p in ORDER:
            gate_up(p, core, group)

    def other(group, arrivals):
        for p in ORDER:
            for k, i in arrivals:
                mate_got[p][k][i].wait_recv()
            gate_up(p, mate, group)

    def rest_of_line(p):
        (a, b, c), *_ = PARTS[p]
        half = me[a] // 2
        buddy = 4 * half + 1 - me[a]
        rest = pl.ds(2 - 2 * half, 2)
        return [ix((a, i), (b, me[b]), (c, me[c])) for i in (buddy, rest)]

    for p in ORDER:
        (a, b, c), *_ = PARTS[p]
        for cp in first_hop[p]:
            cp.wait_recv()
        for cps, k in zip(line[p], (1, 3)):
            cps += [gather(p, at, device(b, k)) for at in rest_of_line(p)]
    for p in ORDER:
        drain(line[p][0] + line[p][1])
        for cps, k in zip(near_got[p][0], (1, 3)):
            cps += [gather(p, at, device(PARTS[p][0][2], k)) for at in rest_of_line(p)]
    for p in ORDER:
        (a, b, c), *_ = PARTS[p]
        up, down = line[p]
        for cp in up:
            cp.wait_recv()
        cps = [gather(p, ix((a, low), (b, off(b, 3)), (c, me[c])), device(b, 1))]
        for cp in down:
            cp.wait_recv()
        cps.append(gather(p, ix((a, high), (b, off(b, 1)), (c, me[c])), device(b, 3)))
        line_far[p] = cps
        spread(p, 1)
    for p in ORDER:
        pass_on(p, 0)
    for p in ORDER:
        (a, b, c), *_ = PARTS[p]
        for cp in line_far[p]:
            cp.wait_recv()
        spread(p, 3)
        mate_got[p][4].append(gather(p, ix((c, me[c])), sister))
    for cp in loads:
        cp.wait()
    plane = [(k, 0) for k in range(SIDE)]
    own(plane)
    for p in ORDER:
        pass_on(p, 1)
        spread(p, 2)
    other(plane, [(4, 0)])
    for k, later in ((0, 3), (1, 2)):
        group = [(k, 1), (k, 3), (k, 2)]
        for p in ORDER:
            far_to_mate(p, k)
        own(group)
        for p in ORDER:
            pass_on(p, later)
        other(group, [(k, 0), (k, 1), (k, 2)])
    group = [(3, 1), (3, 3), (2, 1), (2, 3)]
    own(group)
    for p in ORDER:
        far_to_mate(p, 3)
    other(group, [(3, 0), (3, 1), (2, 0), (2, 1)])
    for p in ORDER:
        far_to_mate(p, 2)
    group = [(3, 2), (2, 2)]
    own(group)
    other(group, [(3, 2), (2, 2)])

    expert = lax.broadcasted_iota(jnp.int32, (256, EXTRA), 1) - local * 2
    hidden_cp = []

    def hide(k):
        i = off(0, k)
        dense = xb1[core, i, :, :, :, 1024:1152].reshape(256, EXTRA).astype(F32)
        for e in range(2):
            weight = jnp.sum(jnp.where(expert == e, dense, 0.0), axis=1, keepdims=True)
            gate = acc[2 * e, i].reshape(256, FFS)
            up = acc[2 * e + 1, i].reshape(256, FFS)
            hidden = gate / (1.0 + jnp.exp(-gate)) * up * weight
            hb[core, i, :, :, :, e * FFS : (e + 1) * FFS] = hidden.astype(BF16).reshape(SIDE, SIDE, ROWS, FFS)
        hidden_cp.append(send(hb.at[core, i], hb.at[core, i], sister))

    def project(p, k):
        (_, b, _), c0, cols, _ = PARTS[p]
        at = ix((b, off(b, k)))

        h = jnp.concatenate([hb[(core_of,) + at].reshape(256, 2 * FFS) for core_of in range(2)], axis=1)
        for n in range(cols // 256):
            w = wd[:, :, :, c0 + n * 256 : c0 + (n + 1) * 256].reshape(4 * FFS, 256)
            r = jnp.dot(h, w, preferred_element_type=F32).astype(BF16)
            ob[p][at + (slice(None), slice(n * 256, (n + 1) * 256))] = r.reshape(SIDE, SIDE, ROWS, 256)

    def add(dst, dst_at, *others):
        total = dst[dst_at].astype(F32)
        for ref, at in others:
            total = total + ref[at].astype(F32)
        dst[dst_at] = total.astype(BF16)

    far_cp = [[None] * 4 for _ in PARTS]
    side_cp = [[[] for _ in range(4)] for _ in PARTS]

    def begin(p, k):
        (a, b, c), *_ = PARTS[p]
        project(p, k)
        bi = off(b, k)

        def to(half, s, into, j):
            return send(ob[p].at[ix((a, half), (b, bi), (c, off(c, s)))], into[p].at[bi, half], device(c, j))

        far_cp[p][k] = (to(low, 2, ro, 1), to(high, 2, ro, 3))
        side_cp[p][k] += [to(high, 1, rp, 1), to(low, 3, rm, 3)]

    def relay(p, k):
        (a, b, c), *_ = PARTS[p]
        bi = off(b, k)
        for cp, half, s, into in zip(far_cp[p][k], (low, high), (1, 3), (rp, rm)):
            cp.wait_recv()
            at = ix((a, half), (b, bi), (c, off(c, s)))
            add(ob[p], at, (ro[p], (bi, half)))
            side_cp[p][k].append(send(ob[p].at[at], into[p].at[bi, half], device(c, s)))

    def settle(p, k):
        (a, b, c), *_ = PARTS[p]
        bi = off(b, k)
        for cp in side_cp[p][k]:
            cp.wait_recv()
        add(ob[p], ix((b, bi), (c, me[c])), (rp[p], bi), (rm[p], bi))

    line_opp, line_cp = [None] * 3, [[] for _ in PARTS]

    def along_b(p, k, half, into, j):
        (a, b, c), *_ = PARTS[p]
        return send(ob[p].at[ix((a, half), (b, off(b, k)), (c, me[c]))], into[p].at[half], device(b, j))

    for k in (2, 1, 3):
        hide(k)
    wd_cp.wait_recv()
    hidden_cp[0].wait_recv()
    begin(2, 2)
    hide(0)
    for cp in hidden_cp[1:]:
        cp.wait_recv()
    for p in (0, 1):
        begin(p, 2)
    for p in (2, 0, 1):
        begin(p, 1)
    for p in (2, 0, 1):
        relay(p, 2)
        begin(p, 3)
    for p in (2, 0, 1):
        relay(p, 1)
        begin(p, 0)
    for p in (2, 0, 1):
        settle(p, 2)
        line_opp[p] = (along_b(p, 2, low, bo, 1), along_b(p, 2, high, bo, 3))
        relay(p, 3)
    for p in (2, 0, 1):
        relay(p, 0)
        settle(p, 1)
        line_cp[p].append(along_b(p, 1, high, bp, 1))
    for p in (2, 0, 1):
        settle(p, 3)
        line_cp[p].append(along_b(p, 3, low, bm, 3))
    for p, ((a, b, c), *_) in enumerate(PARTS):
        line_opp[p][0].wait_recv()
        add(ob[p], ix((a, low), (b, off(b, 1)), (c, me[c])), (bo[p], low))
        line_cp[p].append(along_b(p, 1, low, bp, 1))
        line_opp[p][1].wait_recv()
        add(ob[p], ix((a, high), (b, off(b, 3)), (c, me[c])), (bo[p], high))
        line_cp[p].append(along_b(p, 3, high, bm, 3))
    last = [[] for _ in PARTS]
    for p, ((a, b, c), *_) in enumerate(PARTS):
        settle(p, 0)
        for cp in line_cp[p]:
            cp.wait_recv()
        add(ob[p], ix((b, me[b]), (c, me[c])), (bp[p], slice(None)), (bm[p], slice(None)))
        for k in (1, 2, 3):
            at = ix((a, off(a, k)), (b, me[b]), (c, me[c]))
            last[p].append(send(ob[p].at[at], ra[p].at[k - 1], device(a, k)))
    for p, ((a, b, c), c0, cols, _) in enumerate(PARTS):
        total = ob[p][me].astype(F32)
        for k in (1, 2, 3):
            last[p][k - 1].wait_recv()
            total = total + ra[p][k - 1].astype(F32)
        fin[0, :, c0 : c0 + cols] = total[0:8]
        fin[1, :, c0 : c0 + cols] = total[8:16]
    final = send(fin.at[mate], fin_got, sister)
    final.wait_recv()
    first = core == 0
    mine, got = fin[core], fin_got[...]
    out_ref[:, 0:HALF] = jnp.where(first, mine, got).astype(BF16)
    out_ref[:, HALF : 2 * HALF] = jnp.where(first, got, mine).astype(BF16)
    for cp in copies:
        if not any(cp is other for other in drained):
            cp.wait_send()
    assert len(copies) == N_COPIES


N_COPIES = 238


def body(activations, expert_ids, route_weights, w_gate, w_up, w_down):
    rows, width = activations.shape
    sums = [p[2] for p in PARTS]
    sent = [p[3] for p in PARTS]
    vmem = pltpu.VMEM
    scratch = (
        [vmem((rows, width), BF16), vmem((8, 8), jnp.int32), vmem((8, 8), BF16), vmem((1, 8, HALF + EXTRA), F32), vmem((2, 8, HALF + EXTRA), F32)]
        + [vmem((2, SIDE, SIDE, SIDE, ROWS, w), BF16) for w in sent]
        + [
            vmem((4, 2, HALF, FFS), BF16),
            vmem((2, 2, FFS, HALF), BF16),
            vmem((4, SIDE, SIDE, SIDE, ROWS, FFS), F32),
            vmem((2, SIDE, SIDE, SIDE, ROWS, 2 * FFS), BF16),
        ]
        + [vmem((SIDE, SIDE, SIDE, ROWS, w), BF16) for w in sums]
        + [vmem((SIDE, SIDE, ROWS, w), BF16) for _ in range(3) for w in sums]
        + [vmem((SIDE, ROWS, w), BF16) for _ in range(3) for w in sums]
        + [vmem((3, ROWS, w), BF16) for w in sums]
        + [vmem((2, 8, HALF), F32), vmem((8, HALF), F32)]
        + [pltpu.SemaphoreType.DMA((N_COPIES,)), pltpu.SemaphoreType.DMA((N_COPIES,)), pltpu.SemaphoreType.DMA((9,)), pltpu.SemaphoreType.DMA((3,))]
    )
    in_vmem = pl.BlockSpec(memory_space=pltpu.VMEM)
    in_hbm = pl.BlockSpec(memory_space=pl.ANY)
    return pl.pallas_call(
        kernel,
        out_shape=jax.ShapeDtypeStruct((rows, width), BF16),
        in_specs=[in_hbm] * 6,
        out_specs=in_vmem,
        scratch_shapes=scratch,
        compiler_params=pltpu.CompilerParams(
            collective_id=0, has_side_effects=True, vmem_limit_bytes=62 * 2**20
        ),
        cost_estimate=pl.CostEstimate(flops=2 * 1024 * 7168 * 1536, bytes_accessed=22 * 2**20, transcendentals=2**19),
    )(activations, expert_ids, route_weights, w_gate, w_up, w_down)


def solution(mesh):
    return jax.shard_map(
        body,
        mesh=mesh,
        in_specs=(
            P(("node", "local"), None),
            P(("node", "local"), None),
            P(("node", "local"), None),
            P("local", None, "node"),
            P("local", None, "node"),
            P("local", "node", None),
        ),
        out_specs=P(("node", "local"), None),
        check_vma=False,
    )
```

```python
import jax
import jax.numpy as jnp
from jax import lax
from jax.experimental import pallas as pl
from jax.experimental.pallas import tpu as pltpu
from jax.sharding import PartitionSpec as P

MESH = pl.DeviceIdType.MESH
F32 = jnp.float32
BF16 = jnp.bfloat16

SIDE = 4
ROWS = 16
HALF = 3584
EXTRA = 128
FFS = 256
PARTS = (
    ((0, 1, 2), 0, 1280, 1280),
    ((1, 2, 0), 2560, 1024, 1152),
    ((2, 0, 1), 1280, 1280, 1280),
)
ORDER = (0, 2, 1)


def kernel(
    x_hbm, ids_hbm, rw_hbm, wg_hbm, wu_hbm, wd_hbm, out_ref,
    x_in, ids_in, rw_in, pack, pair, xb0, xb1, xb2, wgu, wd, acc, hb,
    ob0, ob1, ob2, ro0, ro1, ro2, rp0, rp1, rp2, rm0, rm1, rm2,
    bo0, bo1, bo2, bp0, bp1, bp2, bm0, bm1, bm2, ra0, ra1, ra2,
    fin, fin_got, ssem, rsem, lsem, isem,
):
    node = lax.axis_index("node")
    local = lax.axis_index("local")
    core = lax.rem(node, 2)
    me = (local // SIDE, lax.rem(local, SIDE), node // 2)
    mate = 1 - core
    xb, ob = (xb0, xb1, xb2), (ob0, ob1, ob2)
    ro, rp, rm = (ro0, ro1, ro2), (rp0, rp1, rp2), (rm0, rm1, rm2)
    bo, bp, bm, ra = (bo0, bo1, bo2), (bp0, bp1, bp2), (bm0, bm1, bm2), (ra0, ra1, ra2)

    def off(d, k):
        return lax.rem(me[d] + k, SIDE)

    def device(d=None, k=0, other_core=False):
        at = [off(i, k) if i == d else me[i] for i in range(3)]
        return (at[2] * 2 + (mate if other_core else core), at[0] * SIDE + at[1])

    def ix(*pairs):
        at = [slice(None)] * 3
        for d, v in pairs:
            at[d] = v
        return tuple(at)

    copies, drained = [], []

    def drain(cps):
        for cp in cps:
            if not any(cp is other for other in drained):
                cp.wait_send()
                drained.append(cp)

    def send(src, dst, to):
        n = len(copies)
        cp = pltpu.make_async_remote_copy(
            src_ref=src, dst_ref=dst, send_sem=ssem.at[n], recv_sem=rsem.at[n], device_id=to, device_id_type=MESH
        )
        cp.start()
        copies.append(cp)
        return cp

    barrier = pltpu.get_barrier_semaphore()
    peers = [device(other_core=True)] + [device(d, k) for d in range(3) for k in (1, 2, 3)]
    for peer in peers:
        pl.semaphore_signal(barrier, inc=1, device_id=peer, device_id_type=MESH)

    fetches = []
    for n, (src, dst) in enumerate(((x_hbm, x_in), (ids_hbm, ids_in), (rw_hbm, rw_in))):
        fetches.append(pltpu.make_async_copy(src, dst, isem.at[n]))
        fetches[n].start()
    for cp in fetches:
        cp.wait()
    lane = lax.broadcasted_iota(jnp.int32, (8, EXTRA), 1)
    dense = jnp.zeros((8, EXTRA), F32)
    ids = ids_in[...]
    rw = rw_in[...].astype(F32)
    for k in range(8):
        dense = dense + jnp.where(ids[:, k : k + 1] == lane, rw[:, k : k + 1], 0.0)
    pack[0, :, 0:HALF] = x_in[:, pl.ds(pl.multiple_of(mate * HALF, 128), HALF)].astype(F32)
    pack[0, :, HALF : HALF + EXTRA] = dense
    pair[core, :, 0:HALF] = x_in[:, pl.ds(pl.multiple_of(core * HALF, 128), HALF)].astype(F32)
    pair[core, :, HALF : HALF + EXTRA] = dense

    pl.semaphore_wait(barrier, len(peers))
    sister = device(other_core=True)
    swap = send(pack.at[0], pair.at[core], sister)
    swap.wait_recv()
    for p, (_, c0, _, width) in enumerate(PARTS):
        block = pair[:, :, c0 : c0 + width].reshape(ROWS, width)
        xb[p][core, me[0], me[1], me[2]] = block.astype(BF16)

    def gather(p, at, to):
        ref = xb[p].at[(core,) + at]
        return send(ref, ref, to)

    first_hop = [None] * 3
    for p in ORDER:
        (a, b, c), *_ = PARTS[p]
        at = ix((a, me[a]), (b, me[b]), (c, me[c]))
        first_hop[p] = [gather(p, at, device(a, k)) for k in (2, 1, 3)]
    line, line_far = [None] * 3, [None] * 3
    near_got = [[None] * 4 for _ in PARTS]
    for p in ORDER:
        (a, b, c), *_ = PARTS[p]
        at = ix((a, me[a]), (b, me[b]), (c, me[c]))
        line[p] = [[gather(p, at, device(b, k))] for k in (1, 3)]
    for p in ORDER:
        (a, b, c), *_ = PARTS[p]
        at = ix((a, me[a]), (b, me[b]), (c, me[c]))
        near_got[p][0] = [[gather(p, at, device(c, k))] for k in (1, 3)]

    loads = []
    for e in range(2):
        for g, w in enumerate((wg_hbm, wu_hbm)):
            for h in range(2):
                n = len(loads)
                cp = pltpu.make_async_copy(w.at[e, pl.ds(h * HALF, HALF)], wgu.at[2 * e + g, h], lsem.at[n])
                cp.start()
                loads.append(cp)
    own_cols = pl.ds(pl.multiple_of(core * HALF, 128), HALF)
    mate_cols = pl.ds(pl.multiple_of(mate * HALF, 128), HALF)
    cp = pltpu.make_async_copy(wd_hbm.at[:, :, own_cols], wd.at[core], lsem.at[len(loads)])
    cp.start()
    loads.append(cp)

    wd_cp = send(wd_hbm.at[:, :, mate_cols], wd.at[core], sister)
    acc[...] = jnp.zeros_like(acc)

    low, high = pl.ds(0, 2), pl.ds(2, 2)
    far_got = [[None] * 4 for _ in PARTS]
    mate_got = [[[] for _ in range(5)] for _ in PARTS]

    def spread(p, k):
        (a, b, c), *_ = PARTS[p]
        at = ix((b, off(b, k)), (c, me[c]))
        near_got[p][k] = [[gather(p, at, device(c, j))] for j in (1, 3)]

    def pass_on(p, k):
        (a, b, c), *_ = PARTS[p]
        bi = off(b, k)
        cps = []
        for got, half, j, to in zip(near_got[p][k], (low, high), (3, 1), (1, 3)):
            for cp in got:
                cp.wait_recv()
            cps.append(gather(p, ix((a, half), (b, bi), (c, off(c, j))), device(c, to)))
            mate_got[p][k].append(gather(p, ix((b, bi), (c, off(c, j))), sister))
        far_got[p][k] = cps

    def far_to_mate(p, k):
        (a, b, c), *_ = PARTS[p]
        for cp in far_got[p][k]:
            cp.wait_recv()
        mate_got[p][k].append(gather(p, ix((b, off(b, k)), (c, off(c, 2))), sister))

    def gate_up(p, h, group):
        (_, b, c), c0, cols, _ = PARTS[p]
        lines = [ix((b, off(b, kb)), (c, off(c, kc))) for kb, kc in group]
        n = SIDE * ROWS
        x = jnp.concatenate([xb[p][(h,) + at + (slice(None), slice(0, cols))].reshape(n, cols) for at in lines], axis=0)
        for m in range(4):
            r = jnp.dot(x, wgu[m, h, c0 : c0 + cols], preferred_element_type=F32)
            for i, at in enumerate(lines):
                acc[(m,) + at] += r[i * n : (i + 1) * n].reshape(SIDE, ROWS, FFS)

    def own(group):
        for p in ORDER:
            gate_up(p, core, group)

    def other(group, arrivals):
        for p in ORDER:
            for k, i in arrivals:
                mate_got[p][k][i].wait_recv()
            gate_up(p, mate, group)

    def rest_of_line(p):
        (a, b, c), *_ = PARTS[p]
        half = me[a] // 2
        buddy = 4 * half + 1 - me[a]
        rest = pl.ds(2 - 2 * half, 2)
        return [ix((a, i), (b, me[b]), (c, me[c])) for i in (buddy, rest)]

    for p in ORDER:
        (a, b, c), *_ = PARTS[p]
        for cp in first_hop[p]:
            cp.wait_recv()
        for cps, k in zip(line[p], (1, 3)):
            cps += [gather(p, at, device(b, k)) for at in rest_of_line(p)]
    for p in ORDER:
        for cps, k in zip(near_got[p][0], (1, 3)):
            cps += [gather(p, at, device(PARTS[p][0][2], k)) for at in rest_of_line(p)]
    for p in ORDER:
        (a, b, c), *_ = PARTS[p]
        up, down = line[p]
        for cp in up:
            cp.wait_recv()
        cps = [gather(p, ix((a, low), (b, off(b, 3)), (c, me[c])), device(b, 1))]
        for cp in down:
            cp.wait_recv()
        cps.append(gather(p, ix((a, high), (b, off(b, 1)), (c, me[c])), device(b, 3)))
        line_far[p] = cps
        spread(p, 1)
    for p in ORDER:
        pass_on(p, 0)
    for p in ORDER:
        (a, b, c), *_ = PARTS[p]
        for cp in line_far[p]:
            cp.wait_recv()
        spread(p, 3)
        mate_got[p][4].append(gather(p, ix((c, me[c])), sister))
    for cp in loads:
        cp.wait()
    plane = [(k, 0) for k in range(SIDE)]
    own(plane)
    for p in ORDER:
        pass_on(p, 1)
        spread(p, 2)
    other(plane, [(4, 0)])
    for k, later in ((0, 3), (1, 2)):
        group = [(k, 1), (k, 3), (k, 2)]
        for p in ORDER:
            far_to_mate(p, k)
        own(group)
        for p in ORDER:
            pass_on(p, later)
        other(group, [(k, 0), (k, 1), (k, 2)])
    group = [(3, 1), (3, 3), (2, 1), (2, 3)]
    own(group)
    for p in ORDER:
        far_to_mate(p, 3)
    other(group, [(3, 0), (3, 1), (2, 0), (2, 1)])
    for p in ORDER:
        far_to_mate(p, 2)
    group = [(3, 2), (2, 2)]
    own(group)
    other(group, [(3, 2), (2, 2)])

    expert = lax.broadcasted_iota(jnp.int32, (256, EXTRA), 1) - local * 2
    hidden_cp = []
    gathered = list(copies)

    def hide(k):
        i = off(0, k)
        dense = xb1[core, i, :, :, :, 1024:1152].reshape(256, EXTRA).astype(F32)
        for e in range(2):
            weight = jnp.sum(jnp.where(expert == e, dense, 0.0), axis=1, keepdims=True)
            gate = acc[2 * e, i].reshape(256, FFS)
            up = acc[2 * e + 1, i].reshape(256, FFS)
            hidden = gate / (1.0 + jnp.exp(-gate)) * up * weight
            hb[core, i, :, :, :, e * FFS : (e + 1) * FFS] = hidden.astype(BF16).reshape(SIDE, SIDE, ROWS, FFS)
        hidden_cp.append(send(hb.at[core, i], hb.at[core, i], sister))

    def project(p, k, places):
        (_, b, c), c0, cols, _ = PARTS[p]
        lines = [ix((b, off(b, k)), (c, off(c, j))) for j in places]
        n = SIDE * ROWS
        h = jnp.concatenate(
            [jnp.concatenate([hb[(i,) + at].reshape(n, 2 * FFS) for i in range(2)], axis=1) for at in lines], axis=0
        )
        for i in range(cols // 256):
            w = wd[:, :, :, c0 + i * 256 : c0 + (i + 1) * 256].reshape(4 * FFS, 256)
            r = jnp.dot(h, w, preferred_element_type=F32).astype(BF16)
            for j, at in enumerate(lines):
                ob[p][at + (slice(None), slice(i * 256, (i + 1) * 256))] = r[j * n : (j + 1) * n].reshape(SIDE, ROWS, 256)

    def add(dst, dst_at, *others):
        total = dst[dst_at].astype(F32)
        for ref, at in others:
            total = total + ref[at].astype(F32)
        dst[dst_at] = total.astype(BF16)

    far_cp = [[None] * 4 for _ in PARTS]
    side_cp = [[[] for _ in range(4)] for _ in PARTS]

    def begin(p, k, stage=2):
        (a, b, c), *_ = PARTS[p]
        project(p, k, ((2, 0), (1, 3), (2, 1, 3, 0))[stage])
        bi = off(b, k)

        def to(half, s, into, j):
            return send(ob[p].at[ix((a, half), (b, bi), (c, off(c, s)))], into[p].at[bi, half], device(c, j))

        if stage != 1:
            far_cp[p][k] = (to(low, 2, ro, 1), to(high, 2, ro, 3))
        if stage != 0:
            side_cp[p][k] += [to(high, 1, rp, 1), to(low, 3, rm, 3)]

    def relay(p, k):
        (a, b, c), *_ = PARTS[p]
        bi = off(b, k)
        for cp, half, s, into in zip(far_cp[p][k], (low, high), (1, 3), (rp, rm)):
            cp.wait_recv()
            at = ix((a, half), (b, bi), (c, off(c, s)))
            add(ob[p], at, (ro[p], (bi, half)))
            side_cp[p][k].append(send(ob[p].at[at], into[p].at[bi, half], device(c, s)))

    def settle(p, k):
        (a, b, c), *_ = PARTS[p]
        bi = off(b, k)
        for cp in side_cp[p][k]:
            cp.wait_recv()
        add(ob[p], ix((b, bi), (c, me[c])), (rp[p], bi), (rm[p], bi))

    line_opp, line_cp = [None] * 3, [[] for _ in PARTS]

    def along_b(p, k, half, into, j):
        (a, b, c), *_ = PARTS[p]
        return send(ob[p].at[ix((a, half), (b, off(b, k)), (c, me[c]))], into[p].at[half], device(b, j))

    for k in (2, 1, 3):
        hide(k)
    wd_cp.wait_recv()
    hidden_cp[0].wait_recv()
    begin(2, 2, 0)
    hide(0)
    for cp in hidden_cp[1:]:
        cp.wait_recv()
    for p in (0, 1):
        begin(p, 2, 0)
    for p in (2, 0, 1):
        begin(p, 2, 1)
    for p in (2, 0, 1):
        begin(p, 1)
    for p in (2, 0, 1):
        relay(p, 2)
        begin(p, 3)
    for p in (2, 0, 1):
        relay(p, 1)
        begin(p, 0)
    drain(gathered)
    for p in (2, 0, 1):
        settle(p, 2)
        line_opp[p] = (along_b(p, 2, low, bo, 1), along_b(p, 2, high, bo, 3))
        relay(p, 3)
    for p in (2, 0, 1):
        settle(p, 1)
        line_cp[p].append(along_b(p, 1, high, bp, 1))
        relay(p, 0)
    for p in (2, 0, 1):
        settle(p, 3)
        line_cp[p].append(along_b(p, 3, low, bm, 3))
    for p in (2, 0, 1):
        (a, b, c), *_ = PARTS[p]
        line_opp[p][0].wait_recv()
        add(ob[p], ix((a, low), (b, off(b, 1)), (c, me[c])), (bo[p], low))
        line_cp[p].append(along_b(p, 1, low, bp, 1))
        line_opp[p][1].wait_recv()
        add(ob[p], ix((a, high), (b, off(b, 3)), (c, me[c])), (bo[p], high))
        line_cp[p].append(along_b(p, 3, high, bm, 3))
    last = [[] for _ in PARTS]
    for p in (2, 0, 1):
        (a, b, c), *_ = PARTS[p]
        for cp in side_cp[p][0] + line_cp[p]:
            cp.wait_recv()
        every = slice(None)
        add(
            ob[p], ix((b, me[b]), (c, me[c])),
            (rp[p], me[b]), (rm[p], me[b]), (bp[p], every), (bm[p], every),
        )
        for k in (2, 1, 3):
            at = ix((a, off(a, k)), (b, me[b]), (c, me[c]))
            last[p].append(send(ob[p].at[at], ra[p].at[k - 1], device(a, k)))
    drain([cp for cp in copies if not any(cp is other for cps in last for other in cps)])
    for p in (2, 0, 1):
        _, c0, cols, _ = PARTS[p]
        total = ob[p][me].astype(F32)
        for cp in last[p]:
            cp.wait_recv()
        for k in range(3):
            total = total + ra[p][k].astype(F32)
        fin[0, :, c0 : c0 + cols] = total[0:8]
        fin[1, :, c0 : c0 + cols] = total[8:16]
    final = send(fin.at[mate], fin_got, sister)
    drain([cp for cps in last for cp in cps])
    final.wait_recv()
    first = core == 0
    mine, got = fin[core], fin_got[...]
    out_ref[:, 0:HALF] = jnp.where(first, mine, got).astype(BF16)
    out_ref[:, HALF : 2 * HALF] = jnp.where(first, got, mine).astype(BF16)
    drain(copies)
    assert len(copies) == N_COPIES


N_COPIES = 238


def body(activations, expert_ids, route_weights, w_gate, w_up, w_down):
    rows, width = activations.shape
    sums = [p[2] for p in PARTS]
    sent = [p[3] for p in PARTS]
    vmem = pltpu.VMEM
    scratch = (
        [vmem((rows, width), BF16), vmem((8, 8), jnp.int32), vmem((8, 8), BF16), vmem((1, 8, HALF + EXTRA), F32), vmem((2, 8, HALF + EXTRA), F32)]
        + [vmem((2, SIDE, SIDE, SIDE, ROWS, w), BF16) for w in sent]
        + [
            vmem((4, 2, HALF, FFS), BF16),
            vmem((2, 2, FFS, HALF), BF16),
            vmem((4, SIDE, SIDE, SIDE, ROWS, FFS), F32),
            vmem((2, SIDE, SIDE, SIDE, ROWS, 2 * FFS), BF16),
        ]
        + [vmem((SIDE, SIDE, SIDE, ROWS, w), BF16) for w in sums]
        + [vmem((SIDE, SIDE, ROWS, w), BF16) for _ in range(3) for w in sums]
        + [vmem((SIDE, ROWS, w), BF16) for _ in range(3) for w in sums]
        + [vmem((3, ROWS, w), BF16) for w in sums]
        + [vmem((2, 8, HALF), F32), vmem((8, HALF), F32)]
        + [pltpu.SemaphoreType.DMA((N_COPIES,)), pltpu.SemaphoreType.DMA((N_COPIES,)), pltpu.SemaphoreType.DMA((9,)), pltpu.SemaphoreType.DMA((3,))]
    )
    in_vmem = pl.BlockSpec(memory_space=pltpu.VMEM)
    in_hbm = pl.BlockSpec(memory_space=pl.ANY)
    return pl.pallas_call(
        kernel,
        out_shape=jax.ShapeDtypeStruct((rows, width), BF16),
        in_specs=[in_hbm] * 6,
        out_specs=in_vmem,
        scratch_shapes=scratch,
        compiler_params=pltpu.CompilerParams(
            collective_id=0, has_side_effects=True, vmem_limit_bytes=62 * 2**20
        ),
        cost_estimate=pl.CostEstimate(flops=2 * 1024 * 7168 * 1536, bytes_accessed=22 * 2**20, transcendentals=2**19),
    )(activations, expert_ids, route_weights, w_gate, w_up, w_down)


def solution(mesh):
    return jax.shard_map(
        body,
        mesh=mesh,
        in_specs=(
            P(("node", "local"), None),
            P(("node", "local"), None),
            P(("node", "local"), None),
            P("local", None, "node"),
            P("local", None, "node"),
            P("local", "node", None),
        ),
        out_specs=P(("node", "local"), None),
        check_vma=False,
    )
```
